32 devices in a mesh: parts: 2 (over x), rep: 16 (over z, y, core), tp: 1.
Axes of the slice: x: 2, y: 2, z: 4, core: 2. Of those that a mesh axis runs over, the one named last changes fastest.
Arguments:
- hidden: bfloat16 [8192, 8192], P(('parts', 'rep'), 'tp'), parts along dimension 0, may hold values from -6 to 6
- request_adapter: int32 [8192, 1], P(('parts', 'rep')), parts along dimension 0, may hold values from 0 to 31; in each aligned block of 256 rows (0 to 255, 256 to 511, ...) at most 24 rows name the same one
- lengths: int32 [8192], P(('parts', 'rep')), parts along dimension 0, may hold values from 1 to 4096
- key_projection_weight: bfloat16 [8192, 1024], P('tp'), may hold values from -0.0625 to 0.0625
- adapter_down_weight: bfloat16 [32, 8192, 128], P('rep', 'tp'), may hold values from -0.0625 to 0.0625
- adapter_up_weight: bfloat16 [32, 128, 1024], P('rep', None, 'tp'), may hold values from -3 to 3
- slot_adapter_rank: int32 [32], P('rep'), may hold values from 16 to 128, as said below
- placement: int32 [32], replicated, may hold values from 0 to 31, each once
Outputs:
- new_keys: bfloat16 [8192, 1024], P(('parts', 'rep'), 'tp'), parts along dimension 0
The draws below stay inside these ranges and needn't reach their ends.
There are 2 independent parts, one for each index of `parts`. The reference program is written for one: setup_inputs(seed, part) draws one part's arguments, and reference() takes and returns one part's arrays. A program takes and returns all parts, laid end to end along the dimension named above; an argument that names none is the same for every part. Nothing has to cross between parts.
Inputs may be any that keep to these rules, and one draw needn't show every extreme that they name: `slot_adapter_rank`: each slot holds a power of two. `request_adapter`: at most 24 of the 256 requests of one replica name one adapter, a bound that some block reaches of them.
All inputs are finite; a program needn't handle non-finite values.
Results may differ from the reference program's by a relative error of at most 0.0039.
Values may be sent and summed in bfloat16 or wider, within the bound.
A program may use at most 128 MiB of HBM per device.

```python
import math
import jax
import jax.numpy as jnp
import numpy as np
from jax import lax

MODEL_WIDTH = 8192
HEAD = 128
RANK_LIMIT = 128
REQ_DEV = 256
KEY_WIDTH = 1024
ADAPTER_TOTAL = 32
CAP = 24
REQS = 4096
N_REP = 16


def draw_slot_adapter_rank(key, part):
    key = jax.random.fold_in(key, 7)
    first_key, second_key = jax.random.split(key)
    levels = jax.random.randint(first_key, (ADAPTER_TOTAL,), 0, 4)
    levels = levels.at[0].set(0).at[1].set(3)
    levels = levels[jax.random.permutation(second_key, ADAPTER_TOTAL)]
    return (RANK_LIMIT // 2 ** levels).astype(jnp.int32)


def touch_ends(drawn, stream_key, smallest, high):
    spot = [jax.random.randint(jax.random.fold_in(stream_key, axis), (), 0, length) for axis, length in enumerate(drawn.shape)]
    main_axis = drawn.shape.index(max(drawn.shape))
    beside = spot[:main_axis] + [(spot[main_axis] + 1) % drawn.shape[main_axis]] + spot[main_axis + 1:]
    return drawn.at[tuple(spot)].set(smallest).at[tuple(beside)].set(high)


def block_levels(own_key, dims, shards, least, largest):
    def one(position, blocks):
        draws = jax.random.uniform(jax.random.fold_in(jax.random.fold_in(own_key, 6), position), (blocks,), jnp.float32, least / len(shards), largest / len(shards))
        return jnp.repeat(jnp.exp(draws), dims[position] // blocks).reshape((-1,) + (1,) * (len(dims) - position - 1))

    gain = one(*shards[0])
    for cut in shards[1:]:
        gain = gain * one(*cut)
    return gain


def assign_block(stream_key, own, number, rows, amount, top, limit, skew):
    ranking = jax.random.permutation(stream_key, amount)
    crowded, ordinary = portions_of(amount, rows * top, limit, skew, True), portions_of(amount, rows * top, limit, skew, False)
    places = jnp.arange(amount)

    def named(sizes, turn):
        used = int((sizes > 0).sum())
        fixed = max(1, used // 4)
        shifted = fixed + (places - fixed + turn * (used - fixed)) % max(1, amount - fixed)
        return jnp.zeros((amount,), jnp.int32).at[ranking[jnp.where(places < fixed, places, shifted)]].set(jnp.asarray(sizes, jnp.int32))

    sizes = jnp.where(number % 4 == 0, named(crowded, number // 4), named(ordinary, number - number // 4 - 1))
    mixed = jax.random.permutation(jax.random.fold_in(own, 3), amount)
    source_of, taker = mixed[0:amount // 2 * 2:2], mixed[1:amount // 2 * 2:2]
    slack = jnp.minimum(sizes[source_of] - 1, limit - sizes[taker]) // 2
    slack = jnp.where((source_of == ranking[0]) | (taker == ranking[0]) | (sizes[taker] == 0), 0, jnp.maximum(slack, 0))
    shifted = jax.random.randint(jax.random.fold_in(own, 4), (amount // 2,), 0, 1 << 20) % (slack + 1)
    sizes = sizes.at[source_of].add(-shifted).at[taker].add(shifted)
    items = jnp.searchsorted(jnp.cumsum(sizes), jnp.arange(rows * top), side="right").astype(jnp.int32)
    grid = items.reshape(top, rows).T
    grid = grid[jax.random.permutation(jax.random.fold_in(own, 1), rows)]
    turn = jax.random.randint(jax.random.fold_in(own, 2), (rows, 1), 0, top)
    return jnp.take_along_axis(grid, (jnp.arange(top)[None, :] + turn) % top, axis=1)


def portions_of(count, total, bound, skew, full):
    weights = [(1 << 20) // math.isqrt(standing ** skew) + 1 for standing in range(1, count + 1)]
    largest = bound if full else min(bound, max(-(-total // count), total * weights[0] // sum(weights)))
    least = 1 if total - largest >= count - 1 else 0
    holding, surplus = [largest] + [least] * (count - 1), total - largest - least * (count - 1)
    while surplus > 0:
        movable = [i for i in range(1, count) if holding[i] < largest] or [i for i in range(1, count) if holding[i] < bound]
        whole, budget = sum([weights[i] for i in movable]), surplus
        for i in movable:
            addition = min(bound - holding[i], max(1, budget * weights[i] // whole), surplus)
            holding[i] = holding[i] + addition
            surplus = surplus - addition
    return np.array(holding)


def noise(key, extent, width, bound, pieces=(), held_as=jnp.bfloat16):
    result = jax.random.normal(key, extent, jnp.float32) * width
    if len(pieces) > 0:
        result = block_levels(key, extent, pieces, -0.22, 0.18) * result
    return jnp.clip(result, min=-bound, max=bound).astype(held_as)


def setup_inputs(seed: int = 0, part: int = 0) -> dict:
    keys = jax.random.split(jax.random.key(seed), 9)
    own_keys = jax.random.split(jax.random.fold_in(keys[8], part), 9)
    hidden = noise(own_keys[0], (REQS, MODEL_WIDTH), 1.0, 6.0, ((0, 16),))
    request_adapter_keys = jax.random.split(jax.random.fold_in(own_keys[1], 1), REQS // REQ_DEV)
    request_adapter_turns = jax.random.permutation(jax.random.fold_in(own_keys[1], 3), REQS // REQ_DEV)
    request_adapter = jax.vmap(lambda own, number: assign_block(jax.random.fold_in(own_keys[1], 2), own, number, REQ_DEV, ADAPTER_TOTAL, 1, CAP, 2))(request_adapter_keys, request_adapter_turns).reshape((REQS, 1))
    lengths = touch_ends(jax.random.randint(own_keys[2], (REQS,), 1, 4097), jax.random.fold_in(own_keys[2], 1), 1, 4096).astype(jnp.int32)
    key_projection_weight = noise(keys[3], (MODEL_WIDTH, KEY_WIDTH), MODEL_WIDTH ** -0.5, 0.0625)
    adapter_down_weight = noise(keys[4], (ADAPTER_TOTAL, MODEL_WIDTH, RANK_LIMIT), MODEL_WIDTH ** -0.5, 0.0625, ((0, 16),))
    adapter_up_weight = noise(keys[5], (ADAPTER_TOTAL, RANK_LIMIT, KEY_WIDTH), 0.5, 3.0, ((0, 16),))
    slot_adapter_rank = draw_slot_adapter_rank(jax.random.fold_in(keys[8], 71), part)
    placement = jax.random.permutation(keys[7], ADAPTER_TOTAL).astype(jnp.int32)
    return dict(hidden=hidden, request_adapter=request_adapter, lengths=lengths, key_projection_weight=key_projection_weight, adapter_down_weight=adapter_down_weight, adapter_up_weight=adapter_up_weight, slot_adapter_rank=slot_adapter_rank, placement=placement)


def rotary(values, positions, head_size):
    row_count = values.shape[0]
    grouped = values.reshape(row_count, -1, head_size)
    half_size = head_size // 2
    inverse = jnp.exp(jnp.arange(half_size, dtype=jnp.float32) * (-2.0 * math.log(10000.0) / head_size))
    angles = positions.astype(jnp.float32)[:, None] * inverse[None, :]
    cosine = jnp.cos(angles)[:, None, :]
    sine_part = jnp.sin(angles)[:, None, :]
    first_half = grouped[..., :half_size]
    second = grouped[..., half_size:]
    rotated = jnp.concatenate([first_half * cosine - second * sine_part, second * cosine + first_half * sine_part], axis=-1)
    return rotated.reshape(row_count, -1)

def reference(hidden, request_adapter, lengths, key_projection_weight, adapter_down_weight, adapter_up_weight, slot_adapter_rank, placement):
    slot_ids = placement[request_adapter[:, 0]]
    base_key_rows = jnp.dot(hidden, key_projection_weight, preferred_element_type=jnp.float32)
    combined_rows = hidden.shape[0]
    most_rows = CAP * N_REP

    def per_slot(storage_slot_index):
        picked = jnp.nonzero(slot_ids == storage_slot_index, size=most_rows, fill_value=combined_rows)[0].astype(jnp.int32)
        claimed_rows = hidden[jnp.minimum(picked, combined_rows - 1)]
        down_product = jnp.dot(claimed_rows, adapter_down_weight[storage_slot_index], preferred_element_type=jnp.float32)
        rank_now = slot_adapter_rank[storage_slot_index]
        keep_mask = jnp.arange(RANK_LIMIT) < rank_now
        reduced_rank_rows = jnp.where(keep_mask[None, :], down_product * lax.rsqrt(rank_now.astype(jnp.float32)), 0.0).astype(jnp.bfloat16)
        adapter_delta_rows = jnp.dot(reduced_rank_rows, adapter_up_weight[storage_slot_index], preferred_element_type=jnp.float32).astype(jnp.bfloat16)
        return (picked, adapter_delta_rows)
    gathered_weights, delta_values = lax.map(per_slot, jnp.arange(ADAPTER_TOTAL, dtype=jnp.int32))
    adapter_rows = jnp.zeros((combined_rows, KEY_WIDTH), jnp.bfloat16).at[gathered_weights.reshape(-1)].set(delta_values.reshape(-1, KEY_WIDTH), mode='drop')
    key_output_rows = base_key_rows + adapter_rows.astype(jnp.float32)
    return rotary(key_output_rows, lengths, HEAD).astype(jnp.bfloat16)
```

```python
import functools
import math

import jax
import jax.numpy as jnp
from jax import lax
from jax.experimental import pallas as pl
from jax.experimental.pallas import tpu as pltpu
from jax.sharding import PartitionSpec as P

HEAD = 128


def rotary(values, positions, head_size):
    row_count = values.shape[0]
    grouped = values.reshape(row_count, -1, head_size)
    half_size = head_size // 2
    inverse = jnp.exp(
        jnp.arange(half_size, dtype=jnp.float32) * (-2.0 * math.log(10000.0) / head_size)
    )
    angles = positions.astype(jnp.float32)[:, None] * inverse[None, :]
    cosine = jnp.cos(angles)[:, None, :]
    sine_part = jnp.sin(angles)[:, None, :]
    first_half = grouped[..., :half_size]
    second = grouped[..., half_size:]
    rotated = jnp.concatenate(
        [first_half * cosine - second * sine_part, second * cosine + first_half * sine_part],
        axis=-1,
    )
    return rotated.reshape(row_count, -1)


def routed(
    hidden,
    request_adapter,
    lengths,
    key_projection_weight,
    adapter_down_weight,
    adapter_up_weight,
    slot_adapter_rank,
    placement,
):
    row_count = hidden.shape[0]
    feature_half = hidden.shape[1]
    adapter_number = placement.shape[0]
    replica_slot_list = adapter_down_weight.shape[0]
    rank_extent = adapter_down_weight.shape[2]
    key_portion = adapter_up_weight.shape[2]
    replicas = lax.axis_size("rep")
    slot_capacity = 3 * row_count // adapter_number
    table_hit = request_adapter == jnp.arange(adapter_number, dtype=jnp.int32)[None, :]
    slot_ids = jnp.sum(jnp.where(table_hit, placement[None, :], 0), axis=1)
    slot_hit = (slot_ids[:, None] == jnp.arange(adapter_number, dtype=jnp.int32)[None, :]).astype(
        jnp.int32
    )
    within = jnp.sum((jnp.cumsum(slot_hit, axis=0) - 1) * slot_hit, axis=1)
    request_place = slot_ids * slot_capacity + within
    outgoing = (
        jnp.zeros((adapter_number * slot_capacity, feature_half), jnp.bfloat16)
        .at[request_place]
        .set(hidden)
    )
    outgoing = outgoing.reshape(replicas, replica_slot_list, slot_capacity, feature_half)
    rank_scale = lax.rsqrt(slot_adapter_rank.astype(jnp.float32))
    rank_keep = jnp.arange(rank_extent, dtype=jnp.int32)[None, :] < slot_adapter_rank[:, None]
    partial_value = jnp.dot(hidden, key_projection_weight, preferred_element_type=jnp.float32)
    received_rows = lax.all_to_all(outgoing, "rep", split_axis=0, concat_axis=0, tiled=True)
    summed = lax.psum(
        jnp.einsum(
            "khlt,htq->khlq", received_rows, adapter_down_weight, preferred_element_type=jnp.float32
        ),
        "tp",
    )
    reduced_rank_rows = jnp.where(
        rank_keep[None, :, None, :], summed * rank_scale[None, :, None, None], 0.0
    ).astype(jnp.bfloat16)
    sent_back_rows = lax.all_to_all(
        jnp.einsum(
            "pkwb,kbj->pkwj",
            reduced_rank_rows,
            adapter_up_weight,
            preferred_element_type=jnp.float32,
        ).astype(jnp.bfloat16),
        "rep",
        split_axis=0,
        concat_axis=0,
        tiled=True,
    )
    adapter_rows = sent_back_rows.reshape(adapter_number * slot_capacity, key_portion)[
        request_place
    ]
    summed_base = lax.psum(partial_value, "tp")
    replica_portion = lax.dynamic_slice_in_dim(
        summed_base, lax.axis_index("tp") * key_portion, key_portion, 1
    )
    key_output_rows = replica_portion + adapter_rows.astype(jnp.float32)
    return rotary(key_output_rows, lengths, HEAD).astype(jnp.bfloat16)


MESH = pl.DeviceIdType.MESH
LAG = 4


def shrink_kernel(
    n,
    group,
    hidden,
    key_weight,
    down,
    slots,
    shrink,
    base,
    hidden_own,
    key_buf,
    hidden_got,
    slots_got,
    down_got,
    total,
    parts_got,
    h_send,
    h_recv,
    s_send,
    s_recv,
    w_send,
    w_recv,
    f_send,
    f_recv,
    r_send,
    r_recv,
    own_sem,
    key_sem,
):
    part = lax.axis_index("parts")
    me = lax.axis_index("rep")
    place = me % group
    first = me - place
    rows = hidden.shape[0]
    width = hidden.shape[1] // group
    depth = hidden.shape[1] // n
    twin = 1 - part

    def device(p, r):
        return (p, r, 0)

    def cols(j):
        return pl.ds(pl.multiple_of(j * width, width), width)

    def block(j):
        return pl.ds(pl.multiple_of(j * rows, rows), rows)

    barrier = pltpu.get_barrier_semaphore()
    for k in range(1, n):
        pl.semaphore_signal(
            barrier, inc=1, device_id=device(part, (me + k) % n), device_id_type=MESH
        )
    pl.semaphore_signal(barrier, inc=1, device_id=device(twin, me), device_id_type=MESH)

    own_hidden = pltpu.make_async_copy(hidden, hidden_own, own_sem.at[0])
    own_cols = pltpu.make_async_copy(
        hidden.at[:, cols(place)], hidden_got.at[block(place)], own_sem.at[1]
    )
    own_down = pltpu.make_async_copy(
        down.at[:, cols(place)], down_got.at[pl.ds(2 * me, 2)], own_sem.at[2]
    )
    own_slots = pltpu.make_async_copy(slots, slots_got.at[block(place)], own_sem.at[3])

    def key_copy(k):
        at = pl.ds(pl.multiple_of(k * depth, depth), depth)
        return pltpu.make_async_copy(key_weight.at[at], key_buf.at[at], key_sem.at[k])

    def send_hidden(k):
        to = (place + k) % group
        return pltpu.make_async_remote_copy(
            src_ref=hidden.at[:, cols(to)],
            dst_ref=hidden_got.at[block(place)],
            send_sem=h_send.at[k],
            recv_sem=h_recv.at[place],
            device_id=device(part, first + to),
            device_id_type=MESH,
        )

    def send_slots(k):
        to = (place + k) % group
        return pltpu.make_async_remote_copy(
            src_ref=slots,
            dst_ref=slots_got.at[block(place)],
            send_sem=s_send.at[k],
            recv_sem=s_recv.at[place],
            device_id=device(part, first + to),
            device_id_type=MESH,
        )

    def send_down(k):
        to = (me + k) % n
        return pltpu.make_async_remote_copy(
            src_ref=down.at[part, cols(to % group)],
            dst_ref=down_got.at[2 * me + part],
            send_sem=w_send.at[k],
            recv_sem=w_recv.at[me],
            device_id=device(part, to),
            device_id_type=MESH,
        )

    def pass_on(k):
        source = (me + n - k) % n
        return pltpu.make_async_remote_copy(
            src_ref=down_got.at[2 * source + part],
            dst_ref=down_got.at[2 * source + part],
            send_sem=f_send.at[k],
            recv_sem=f_recv.at[k],
            device_id=device(twin, me),
            device_id_type=MESH,
        )

    def got_hidden(k):
        source = (place + k) % group
        return pltpu.make_async_remote_copy(
            src_ref=hidden.at[:, cols(place)],
            dst_ref=hidden_got.at[block(source)],
            send_sem=h_send.at[k],
            recv_sem=h_recv.at[source],
            device_id=device(part, first + source),
            device_id_type=MESH,
        )

    def got_slots(k):
        source = (place + k) % group
        return pltpu.make_async_remote_copy(
            src_ref=slots,
            dst_ref=slots_got.at[block(source)],
            send_sem=s_send.at[k],
            recv_sem=s_recv.at[source],
            device_id=device(part, first + source),
            device_id_type=MESH,
        )

    def got_down(k):
        source = (me + n - k) % n
        return pltpu.make_async_remote_copy(
            src_ref=down.at[part, cols(place)],
            dst_ref=down_got.at[2 * source + part],
            send_sem=w_send.at[k],
            recv_sem=w_recv.at[source],
            device_id=device(part, source),
            device_id_type=MESH,
        )

    def got_passed(k):
        source = (me + n - k) % n
        return pltpu.make_async_remote_copy(
            src_ref=down_got.at[2 * source + twin],
            dst_ref=down_got.at[2 * source + twin],
            send_sem=f_send.at[k],
            recv_sem=f_recv.at[k],
            device_id=device(twin, me),
            device_id_type=MESH,
        )

    own_hidden.start()
    for k in range(n):
        key_copy(k).start()
    own_down.start()
    own_cols.start()
    own_slots.start()
    pl.semaphore_wait(barrier, n)
    for k in range(1, group):
        send_slots(k).start()
    for k in range(1, n):
        send_down(k).start()
        if k < group:
            send_hidden(k).start()

    total[...] = jnp.zeros_like(total)
    base[...] = jnp.zeros_like(base)
    own_hidden.wait()

    def base_step(k):
        key_copy(k).wait()
        at = pl.ds(pl.multiple_of(k * depth, depth), depth)
        base[...] += jnp.dot(
            hidden_own[:, at], key_buf[at, :], preferred_element_type=jnp.float32
        )

    def shrink_step(k):
        source = (me + n - k) % n
        low_slot = (2 * source).astype(jnp.float32)

        def tile(j, carry):
            at = block(j)
            weight = jnp.concatenate([down_got[2 * source], down_got[2 * source + 1]], axis=1)
            product = jnp.dot(hidden_got[at, :], weight, preferred_element_type=jnp.float32)
            slot = slots_got[at, :].astype(jnp.float32)
            half = product.shape[1] // 2
            total[at, :] = jnp.where(
                slot == low_slot,
                product[:, :half],
                jnp.where(slot == low_slot + 1.0, product[:, half:], total[at, :]),
            )
            return carry

        lax.fori_loop(0, group, tile, 0)

    base_step(0)

    def early(k, carry):
        got_down(k).wait_recv()
        pass_on(k).start()
        base_step(k)
        return carry

    def middle(k, carry):
        got_down(k).wait_recv()
        pass_on(k).start()
        base_step(k)
        got_passed(k - LAG).wait_recv()
        shrink_step(k - LAG)
        return carry

    def late(k, carry):
        got_passed(k).wait_recv()
        shrink_step(k)
        return carry

    lax.fori_loop(1, LAG + 1, early, 0)
    own_cols.wait()
    own_down.wait()
    own_slots.wait()
    for k in range(1, group):
        got_slots(k).wait_recv()
        got_hidden(k).wait_recv()
    shrink_step(0)
    lax.fori_loop(LAG + 1, n, middle, 0)
    lax.fori_loop(n - LAG, n, late, 0)

    def send_total(k):
        to = (place + k) % group
        return pltpu.make_async_remote_copy(
            src_ref=total.at[block(to)],
            dst_ref=parts_got.at[place],
            send_sem=r_send.at[k],
            recv_sem=r_recv.at[place],
            device_id=device(part, first + to),
            device_id_type=MESH,
        )

    def got_total(k):
        source = (place + k) % group
        return pltpu.make_async_remote_copy(
            src_ref=total.at[block(place)],
            dst_ref=parts_got.at[source],
            send_sem=r_send.at[k],
            recv_sem=r_recv.at[source],
            device_id=device(part, first + source),
            device_id_type=MESH,
        )

    for k in range(1, group):
        send_total(k).start()
    summed = total[block(place), :]
    for k in range(1, group):
        got_total(k).wait_recv()
        summed = summed + parts_got[(place + k) % group]
    shrink[...] = summed

    for k in range(1, group):
        send_slots(k).wait_send()
        send_hidden(k).wait_send()
        send_total(k).wait_send()
    for k in range(1, n):
        send_down(k).wait_send()
        pass_on(k).wait_send()


def shrink_and_base(hidden, key_weight, down, slots):
    n = lax.axis_size("rep")
    group = n // 2
    rows, features = hidden.shape
    rank_extent = down.shape[2]
    width = features // group
    keys = key_weight.shape[1]
    any_space = pl.BlockSpec(memory_space=pl.ANY)
    vmem = pl.BlockSpec(memory_space=pltpu.VMEM)
    dma = pltpu.SemaphoreType.DMA
    return pl.pallas_call(
        functools.partial(shrink_kernel, n, group),
        out_shape=(
            jax.ShapeDtypeStruct((rows, rank_extent), jnp.float32),
            jax.ShapeDtypeStruct((rows, keys), jnp.float32),
        ),
        in_specs=[any_space] * 4,
        out_specs=(vmem, vmem),
        scratch_shapes=[
            pltpu.VMEM((rows, features), jnp.bfloat16),
            pltpu.VMEM((features, keys), jnp.bfloat16),
            pltpu.VMEM((group * rows, width), jnp.bfloat16),
            pltpu.VMEM((group * rows, rank_extent), jnp.bfloat16),
            pltpu.VMEM((2 * n, width, rank_extent), jnp.bfloat16),
            pltpu.VMEM((group * rows, rank_extent), jnp.float32),
            pltpu.VMEM((group, rows, rank_extent), jnp.float32),
            dma((group,)),
            dma((group,)),
            dma((group,)),
            dma((group,)),
            dma((n,)),
            dma((n,)),
            dma((n,)),
            dma((n,)),
            dma((group,)),
            dma((group,)),
            dma((4,)),
            dma((n,)),
        ],
        compiler_params=pltpu.CompilerParams(
            collective_id=0, has_side_effects=True, vmem_limit_bytes=56 * 2**20
        ),
        cost_estimate=pl.CostEstimate(
            flops=2 * rows * features * keys + 4 * rows * features * n * rank_extent,
            bytes_accessed=2 * features * (rows + keys + 2 * rank_extent),
            transcendentals=0,
        ),
    )(hidden, key_weight, down, slots)


def shared(
    hidden,
    request_adapter,
    lengths,
    key_projection_weight,
    adapter_down_weight,
    adapter_up_weight,
    slot_adapter_rank,
    placement,
):
    rows = hidden.shape[0]
    adapters = placement.shape[0]
    rank_extent = adapter_down_weight.shape[2]
    numbers = jnp.arange(adapters, dtype=jnp.int32)[None, :]
    slot_ids = jnp.sum(jnp.where(request_adapter == numbers, placement[None, :], 0), axis=1)
    slot_hit = slot_ids[:, None] == numbers
    slots = jnp.broadcast_to(slot_ids[:, None].astype(jnp.bfloat16), (rows, rank_extent))
    all_up = lax.all_gather(adapter_up_weight, "rep", tiled=True)
    all_ranks = lax.all_gather(slot_adapter_rank, "rep", tiled=True)
    shrink, base = shrink_and_base(hidden, key_projection_weight, adapter_down_weight, slots)
    rank = jnp.sum(jnp.where(slot_hit, all_ranks[None, :], 0), axis=1)[:, None]
    keep = jnp.arange(rank_extent, dtype=jnp.int32)[None, :] < rank
    low = jnp.where(keep, shrink * lax.rsqrt(rank.astype(jnp.float32)), 0.0).astype(jnp.bfloat16)
    spread = jnp.where(slot_hit[:, :, None], low[:, None, :], jnp.bfloat16(0))
    delta = jnp.dot(
        spread.reshape(rows, adapters * rank_extent),
        all_up.reshape(adapters * rank_extent, -1),
        preferred_element_type=jnp.float32,
    ).astype(jnp.bfloat16)
    return rotary(base + delta.astype(jnp.float32), lengths, HEAD).astype(jnp.bfloat16)


def solution(mesh):
    sizes = dict(mesh.shape)
    fits = sizes["parts"] == 2 and sizes["tp"] == 1 and sizes["rep"] % 8 == 0
    on_device = shared if fits else routed
    in_specs = (
        P(("parts", "rep"), "tp"),
        P(("parts", "rep"), None),
        P(("parts", "rep")),
        P("tp", None),
        P("rep", "tp", None),
        P("rep", None, "tp"),
        P("rep"),
        P(),
    )
    out_specs = P(("parts", "rep"), "tp")
    return jax.shard_map(
        on_device, mesh=mesh, in_specs=in_specs, out_specs=out_specs, check_vma=False
    )
```

```python
import functools
import math

import jax
import jax.numpy as jnp
from jax import lax
from jax.experimental import pallas as pl
from jax.experimental.pallas import tpu as pltpu
from jax.sharding import PartitionSpec as P

HEAD = 128


def rotary(values, positions, head_size):
    row_count = values.shape[0]
    grouped = values.reshape(row_count, -1, head_size)
    half_size = head_size // 2
    inverse = jnp.exp(
        jnp.arange(half_size, dtype=jnp.float32) * (-2.0 * math.log(10000.0) / head_size)
    )
    angles = positions.astype(jnp.float32)[:, None] * inverse[None, :]
    cosine = jnp.cos(angles)[:, None, :]
    sine_part = jnp.sin(angles)[:, None, :]
    first_half = grouped[..., :half_size]
    second = grouped[..., half_size:]
    rotated = jnp.concatenate(
        [first_half * cosine - second * sine_part, second * cosine + first_half * sine_part],
        axis=-1,
    )
    return rotated.reshape(row_count, -1)


def routed(
    hidden,
    request_adapter,
    lengths,
    key_projection_weight,
    adapter_down_weight,
    adapter_up_weight,
    slot_adapter_rank,
    placement,
):
    row_count = hidden.shape[0]
    feature_half = hidden.shape[1]
    adapter_number = placement.shape[0]
    replica_slot_list = adapter_down_weight.shape[0]
    rank_extent = adapter_down_weight.shape[2]
    key_portion = adapter_up_weight.shape[2]
    replicas = lax.axis_size("rep")
    slot_capacity = 3 * row_count // adapter_number
    table_hit = request_adapter == jnp.arange(adapter_number, dtype=jnp.int32)[None, :]
    slot_ids = jnp.sum(jnp.where(table_hit, placement[None, :], 0), axis=1)
    slot_hit = (slot_ids[:, None] == jnp.arange(adapter_number, dtype=jnp.int32)[None, :]).astype(
        jnp.int32
    )
    within = jnp.sum((jnp.cumsum(slot_hit, axis=0) - 1) * slot_hit, axis=1)
    request_place = slot_ids * slot_capacity + within
    outgoing = (
        jnp.zeros((adapter_number * slot_capacity, feature_half), jnp.bfloat16)
        .at[request_place]
        .set(hidden)
    )
    outgoing = outgoing.reshape(replicas, replica_slot_list, slot_capacity, feature_half)
    rank_scale = lax.rsqrt(slot_adapter_rank.astype(jnp.float32))
    rank_keep = jnp.arange(rank_extent, dtype=jnp.int32)[None, :] < slot_adapter_rank[:, None]
    partial_value = jnp.dot(hidden, key_projection_weight, preferred_element_type=jnp.float32)
    received_rows = lax.all_to_all(outgoing, "rep", split_axis=0, concat_axis=0, tiled=True)
    summed = lax.psum(
        jnp.einsum(
            "khlt,htq->khlq", received_rows, adapter_down_weight, preferred_element_type=jnp.float32
        ),
        "tp",
    )
    reduced_rank_rows = jnp.where(
        rank_keep[None, :, None, :], summed * rank_scale[None, :, None, None], 0.0
    ).astype(jnp.bfloat16)
    sent_back_rows = lax.all_to_all(
        jnp.einsum(
            "pkwb,kbj->pkwj",
            reduced_rank_rows,
            adapter_up_weight,
            preferred_element_type=jnp.float32,
        ).astype(jnp.bfloat16),
        "rep",
        split_axis=0,
        concat_axis=0,
        tiled=True,
    )
    adapter_rows = sent_back_rows.reshape(adapter_number * slot_capacity, key_portion)[
        request_place
    ]
    summed_base = lax.psum(partial_value, "tp")
    replica_portion = lax.dynamic_slice_in_dim(
        summed_base, lax.axis_index("tp") * key_portion, key_portion, 1
    )
    key_output_rows = replica_portion + adapter_rows.astype(jnp.float32)
    return rotary(key_output_rows, lengths, HEAD).astype(jnp.bfloat16)


MESH = pl.DeviceIdType.MESH
WINDOW = 4
TILE = 1024
TURN = 9


def flip(index, mask):
    out = 0
    for bit in (1, 2, 4, 8):
        out = out + (index // bit % 2 + mask // bit % 2) % 2 * bit
    return out


def mask_at(k):
    return k % 2 * (8 + k // 2) + (1 - k % 2) * ((k // 2 * 4 + 6) % 7 + 1)


def keys_kernel(
    n,
    group,
    hidden,
    key_weight,
    down,
    up,
    slots,
    cosine,
    sine,
    out,
    hidden_own,
    key_buf,
    hidden_got,
    slots_got,
    down_got,
    up_got,
    base,
    total,
    totals_got,
    low_got,
    delta,
    delta_got,
    h_send,
    h_recv,
    s_send,
    s_recv,
    d_send,
    d_recv,
    dp_send,
    dp_recv,
    u_send,
    u_recv,
    up_send,
    up_recv,
    t_send,
    t_recv,
    l_send,
    l_recv,
    e_send,
    e_recv,
    own_sem,
    key_sem,
):
    part = lax.axis_index("parts")
    me = lax.axis_index("rep")
    twin = 1 - part
    place = me % group
    first = me - place
    rows, features = hidden.shape
    rank_extent = down.shape[2]
    width = features // group
    depth = features // n
    keys = key_weight.shape[1] // group

    def part_of(j, size):
        return pl.ds(pl.multiple_of(j * size, size), size)

    def remote(source, target, send, recv, p, r):
        return pltpu.make_async_remote_copy(
            src_ref=source,
            dst_ref=target,
            send_sem=send,
            recv_sem=recv,
            device_id=(p, r, 0),
            device_id_type=MESH,
        )

    def hidden_copy(k, to, who, other):
        return remote(
            hidden.at[:, part_of(to % group, width)],
            hidden_got.at[part_of(who % group, rows)],
            h_send.at[k],
            h_recv.at[k],
            part,
            other,
        )

    def slots_copy(k, to, who, other):
        return remote(
            slots,
            slots_got.at[part_of(who % group, rows)],
            s_send.at[k],
            s_recv.at[k],
            part,
            other,
        )

    def down_copy(k, to, who, other):
        return remote(
            down.at[part, part_of(to % group, width)],
            down_got.at[2 * who + part],
            d_send.at[k],
            d_recv.at[k],
            part,
            other,
        )

    def near_copy(k, to, who, other):
        return remote(
            down.at[:, part_of(to % group, width)],
            down_got.at[pl.ds(2 * who, 2)],
            d_send.at[k],
            d_recv.at[k],
            part,
            other,
        )

    def up_copy(k, to, who, other):
        return remote(
            up.at[part, :, part_of(to % group, keys)],
            up_got.at[2 * who + part],
            u_send.at[k],
            u_recv.at[k],
            part,
            other,
        )

    def total_copy(k, to, who, other):
        return remote(
            total.at[part_of(to % group, rows)],
            totals_got.at[who % group],
            t_send.at[k],
            t_recv.at[k],
            part,
            other,
        )

    def low_copy(k, to, who, other):
        return remote(
            low_got.at[who % group],
            low_got.at[who % group],
            l_send.at[k],
            l_recv.at[k],
            part,
            other,
        )

    def delta_copy(k, to, who, other):
        return remote(
            delta.at[to % group],
            delta_got.at[who % group],
            e_send.at[k],
            e_recv.at[k],
            part,
            other,
        )

    def sent(copy, k):
        other = flip(me, k)
        return copy(k, other, me, other)

    def coming(copy, k):
        other = flip(me, k)
        return copy(k, me, other, other)

    def down_pass(k, slot_part):
        at = down_got.at[2 * flip(me, k) + slot_part]
        return remote(at, at, dp_send.at[k], dp_recv.at[k], twin, me)

    def up_pass(k, slot_part):
        at = up_got.at[2 * flip(me, k) + slot_part]
        return remote(at, at, up_send.at[k], up_recv.at[k], twin, me)

    def key_copy(k):
        at = part_of(k, depth)
        return pltpu.make_async_copy(key_weight.at[at], key_buf.at[at], key_sem.at[k])

    barrier = pltpu.get_barrier_semaphore()
    for k in range(1, n):
        pl.semaphore_signal(
            barrier, inc=1, device_id=(part, flip(me, k), 0), device_id_type=MESH
        )
    pl.semaphore_signal(barrier, inc=1, device_id=(twin, me, 0), device_id_type=MESH)

    own = [
        pltpu.make_async_copy(hidden, hidden_own, own_sem.at[0]),
        pltpu.make_async_copy(
            hidden.at[:, part_of(place, width)],
            hidden_got.at[part_of(place, rows)],
            own_sem.at[1],
        ),
        pltpu.make_async_copy(
            down.at[:, part_of(place, width)], down_got.at[pl.ds(2 * me, 2)], own_sem.at[2]
        ),
        pltpu.make_async_copy(
            up.at[:, :, part_of(place, keys)], up_got.at[pl.ds(2 * me, 2)], own_sem.at[3]
        ),
        pltpu.make_async_copy(slots, slots_got.at[part_of(place, rows)], own_sem.at[4]),
    ]
    pl.semaphore_wait(barrier, n)
    for k in range(1, WINDOW + 1):
        sent(down_copy if k % 4 else near_copy, mask_at(k)).start()
    for k in (1, 2, 3):
        sent(hidden_copy, k).start()
    for k in range(1, group):
        sent(slots_copy, k).start()
    for copy in own:
        copy.start()
    for k in range(n):
        key_copy(k).start()

    total[...] = jnp.zeros_like(total)
    base[...] = jnp.zeros_like(base)

    def base_step(k):
        key_copy(k).wait()
        at = part_of(k, depth)
        base[...] += jnp.dot(
            hidden_own[:, at], key_buf[at, :], preferred_element_type=jnp.float32
        )

    def pass_down(k):
        mask = mask_at(k)

        @pl.when(k % 4 > 0)
        def _():
            coming(down_copy, mask).wait_recv()
            down_pass(mask, part).start()

        @pl.when(k % 4 == 0)
        def _():
            coming(near_copy, mask).wait_recv()

        later = k + WINDOW

        @pl.when((later < n) & (later % 4 > 0))
        def _():
            sent(down_copy, mask_at(later)).start()

        @pl.when((later < n) & (later % 4 == 0))
        def _():
            sent(near_copy, mask_at(later)).start()

        base_step(k)

    def shrink_pair(s):
        low_slot = (2 * s).astype(jnp.float32)

        def tile(j, carry):
            at = part_of(j, TILE)
            slot = slots_got[at, :].astype(jnp.float32)
            weight = jnp.concatenate([down_got[2 * s], down_got[2 * s + 1]], axis=1)
            product = jnp.dot(hidden_got[at, :], weight, preferred_element_type=jnp.float32)
            total[at, :] = jnp.where(
                slot == low_slot,
                product[:, :rank_extent],
                jnp.where(slot == low_slot + 1.0, product[:, rank_extent:], total[at, :]),
            )
            return carry

        lax.fori_loop(0, group * rows // TILE, tile, 0)

    def shrink_step(k, carry):
        mask = mask_at(k)

        @pl.when(k % 4 > 0)
        def _():
            down_pass(mask, twin).wait_recv()

        shrink_pair(flip(me, mask))
        return carry

    def first_steps(k, carry):
        pass_down(k)

        @pl.when(k % 2 * (8 // (k + 1)) >= 1)
        def _():
            sent(hidden_copy, 4 + k // 2).start()

        return carry

    def last_steps(k, carry):
        pass_down(k)
        shrink_step(2 * (k - TURN) - 1, 0)
        shrink_step(2 * (k - TURN), 0)
        return carry

    own[0].wait()
    base_step(0)
    lax.fori_loop(1, TURN + 1, first_steps, 0)
    for k in range(1, n):
        sent(up_copy, k).start()
    for copy in own[1:]:
        copy.wait()
    for k in range(1, group):
        coming(slots_copy, k).wait_recv()
        coming(hidden_copy, k).wait_recv()
    shrink_pair(me)
    lax.fori_loop(TURN + 1, n, last_steps, 0)
    lax.fori_loop(2 * (n - 1 - TURN) + 1, n, shrink_step, 0)
    for k in range(1, group):
        sent(total_copy, k).start()

    def pass_up(k, carry):
        mask = mask_at(k)
        coming(up_copy, mask).wait_recv()
        up_pass(mask, part).start()
        return carry

    lax.fori_loop(1, n, pass_up, 0)

    def wait_passed_up(k, carry):
        up_pass(mask_at(k), twin).wait_recv()
        return carry

    lax.fori_loop(1, n, wait_passed_up, 0)

    own_slot = slots_got[part_of(place, rows), :].astype(jnp.float32)

    def find_rank(s, rank):
        here = up_got[s, rank_extent : rank_extent + 16, :].astype(jnp.float32)[0:1, :]
        return jnp.where(own_slot == s.astype(jnp.float32), here, rank)

    rank = lax.fori_loop(0, 2 * n, find_rank, jnp.ones((rows, rank_extent), jnp.float32))
    feature = lax.broadcasted_iota(jnp.int32, (rows, rank_extent), 1).astype(jnp.float32)
    shrink = total[part_of(place, rows), :]
    for k in range(1, group):
        coming(total_copy, k).wait_recv()
        shrink = shrink + totals_got[flip(place, k)]
    low_got[place] = jnp.where(feature < rank, shrink * lax.rsqrt(rank), 0.0).astype(jnp.bfloat16)
    for k in range(1, group):
        sent(low_copy, k).start()

    def expand_block(j):
        slot = slots_got[part_of(j, rows), :].astype(jnp.float32)
        low = low_got[j].astype(jnp.float32)

        def pair(s, sum_so_far):
            low_slot = (2 * s).astype(jnp.float32)
            spread = jnp.concatenate(
                [
                    jnp.where(slot == low_slot, low, 0.0).astype(jnp.bfloat16),
                    jnp.where(slot == low_slot + 1.0, low, 0.0).astype(jnp.bfloat16),
                ],
                axis=1,
            )
            weight = jnp.concatenate(
                [up_got[2 * s, :rank_extent, :], up_got[2 * s + 1, :rank_extent, :]], axis=0
            )
            return sum_so_far + jnp.dot(spread, weight, preferred_element_type=jnp.float32)

        delta[j] = lax.fori_loop(
            0, n, pair, jnp.zeros((rows, keys), jnp.float32), unroll=4
        ).astype(jnp.bfloat16)

    def expand_step(k, carry):
        coming(low_copy, k).wait_recv()
        expand_block(flip(place, k))
        sent(delta_copy, k).start()
        return carry

    def rotate(j, values):
        at = part_of(j, keys)
        pre = base[:, at] + values.astype(jnp.float32)
        turned = pltpu.roll(pre, keys // 2, axis=1)
        out[:, at] = (pre * cosine[...] + turned * sine[...]).astype(out.dtype)

    def rotate_step(k, carry):
        coming(delta_copy, k).wait_recv()
        j = flip(place, k)
        rotate(j, delta_got[j])
        return carry

    lax.fori_loop(1, group, expand_step, 0)
    expand_block(place)
    rotate(place, delta[place])
    lax.fori_loop(1, group, rotate_step, 0)

    for k in range(1, group):
        for copy in (hidden_copy, slots_copy, total_copy, low_copy, delta_copy):
            sent(copy, k).wait_send()
    for k in range(1, n):
        if k < 4:
            sent(near_copy, k).wait_send()
        else:
            sent(down_copy, k).wait_send()
            down_pass(k, part).wait_send()
        sent(up_copy, k).wait_send()
        up_pass(k, part).wait_send()


def keys_call(hidden, key_weight, down, up, slots, cosine, sine):
    n = lax.axis_size("rep")
    group = n // 2
    rows, features = hidden.shape
    rank_extent = down.shape[2]
    width = features // group
    keys = key_weight.shape[1]
    key_block = keys // group
    any_space = pl.BlockSpec(memory_space=pl.ANY)
    vmem = pl.BlockSpec(memory_space=pltpu.VMEM)
    half, full = jnp.bfloat16, jnp.float32
    dma = pltpu.SemaphoreType.DMA
    return pl.pallas_call(
        functools.partial(keys_kernel, n, group),
        out_shape=jax.ShapeDtypeStruct((rows, keys), half),
        in_specs=[any_space] * 5 + [vmem] * 2,
        out_specs=vmem,
        scratch_shapes=[
            pltpu.VMEM((rows, features), half),
            pltpu.VMEM((features, keys), half),
            pltpu.VMEM((group * rows, width), half),
            pltpu.VMEM((group * rows, rank_extent), half),
            pltpu.VMEM((2 * n, width, rank_extent), half),
            pltpu.VMEM((2 * n, up.shape[1], key_block), half),
            pltpu.VMEM((rows, keys), full),
            pltpu.VMEM((group * rows, rank_extent), full),
            pltpu.VMEM((group, rows, rank_extent), full),
            pltpu.VMEM((group, rows, rank_extent), half),
            pltpu.VMEM((group, rows, key_block), half),
            pltpu.VMEM((group, rows, key_block), half),
        ]
        + [dma((group,))] * 4
        + [dma((n,))] * 8
        + [dma((group,))] * 6
        + [dma((5,)), dma((n,))],
        compiler_params=pltpu.CompilerParams(
            collective_id=0, has_side_effects=True, vmem_limit_bytes=56 * 2**20
        ),
        cost_estimate=pl.CostEstimate(
            flops=2 * rows * features * keys + 4 * rows * features * n * rank_extent,
            bytes_accessed=2 * features * (rows + keys + 2 * rank_extent),
            transcendentals=0,
        ),
    )(hidden, key_weight, down, up, slots, cosine, sine)


def shared(
    hidden,
    request_adapter,
    lengths,
    key_projection_weight,
    adapter_down_weight,
    adapter_up_weight,
    slot_adapter_rank,
    placement,
):
    rows = hidden.shape[0]
    adapters = placement.shape[0]
    rank_extent = adapter_down_weight.shape[2]
    numbers = jnp.arange(adapters, dtype=jnp.int32)[None, :]
    slot_ids = jnp.sum(jnp.where(request_adapter == numbers, placement[None, :], 0), axis=1)
    slots = jnp.broadcast_to(slot_ids[:, None].astype(jnp.bfloat16), (rows, rank_extent))
    ranks = jnp.broadcast_to(
        slot_adapter_rank.astype(jnp.bfloat16)[:, None, None],
        (slot_adapter_rank.shape[0], 16, adapter_up_weight.shape[2]),
    )
    up = jnp.concatenate([adapter_up_weight, ranks], axis=1)
    half_size = HEAD // 2
    inverse = jnp.exp(
        jnp.arange(half_size, dtype=jnp.float32) * (-2.0 * math.log(10000.0) / HEAD)
    )
    angles = lengths.astype(jnp.float32)[:, None] * inverse[None, :]
    cosine, sine = jnp.cos(angles), jnp.sin(angles)
    return keys_call(
        hidden,
        key_projection_weight,
        adapter_down_weight,
        up,
        slots,
        jnp.concatenate([cosine, cosine], axis=1),
        jnp.concatenate([-sine, sine], axis=1),
    )


def solution(mesh):
    sizes = dict(mesh.shape)
    fits = sizes["parts"] == 2 and sizes["tp"] == 1 and sizes["rep"] == 16
    on_device = shared if fits else routed
    in_specs = (
        P(("parts", "rep"), "tp"),
        P(("parts", "rep"), None),
        P(("parts", "rep")),
        P("tp", None),
        P("rep", "tp", None),
        P("rep", None, "tp"),
        P("rep"),
        P(),
    )
    out_specs = P(("parts", "rep"), "tp")
    return jax.shard_map(
        on_device, mesh=mesh, in_specs=in_specs, out_specs=out_specs, check_vma=False
    )
```

```python
import functools
import math

import jax
import jax.numpy as jnp
from jax import lax
from jax.experimental import pallas as pl
from jax.experimental.pallas import tpu as pltpu
from jax.sharding import PartitionSpec as P

HEAD = 128


def rotary(values, positions, head_size):
    row_count = values.shape[0]
    grouped = values.reshape(row_count, -1, head_size)
    half_size = head_size // 2
    inverse = jnp.exp(
        jnp.arange(half_size, dtype=jnp.float32) * (-2.0 * math.log(10000.0) / head_size)
    )
    angles = positions.astype(jnp.float32)[:, None] * inverse[None, :]
    cosine = jnp.cos(angles)[:, None, :]
    sine_part = jnp.sin(angles)[:, None, :]
    first_half = grouped[..., :half_size]
    second = grouped[..., half_size:]
    rotated = jnp.concatenate(
        [first_half * cosine - second * sine_part, second * cosine + first_half * sine_part],
        axis=-1,
    )
    return rotated.reshape(row_count, -1)


def routed(
    hidden,
    request_adapter,
    lengths,
    key_projection_weight,
    adapter_down_weight,
    adapter_up_weight,
    slot_adapter_rank,
    placement,
):
    row_count = hidden.shape[0]
    feature_half = hidden.shape[1]
    adapter_number = placement.shape[0]
    replica_slot_list = adapter_down_weight.shape[0]
    rank_extent = adapter_down_weight.shape[2]
    key_portion = adapter_up_weight.shape[2]
    replicas = lax.axis_size("rep")
    slot_capacity = 3 * row_count // adapter_number
    table_hit = request_adapter == jnp.arange(adapter_number, dtype=jnp.int32)[None, :]
    slot_ids = jnp.sum(jnp.where(table_hit, placement[None, :], 0), axis=1)
    slot_hit = (slot_ids[:, None] == jnp.arange(adapter_number, dtype=jnp.int32)[None, :]).astype(
        jnp.int32
    )
    within = jnp.sum((jnp.cumsum(slot_hit, axis=0) - 1) * slot_hit, axis=1)
    request_place = slot_ids * slot_capacity + within
    outgoing = (
        jnp.zeros((adapter_number * slot_capacity, feature_half), jnp.bfloat16)
        .at[request_place]
        .set(hidden)
    )
    outgoing = outgoing.reshape(replicas, replica_slot_list, slot_capacity, feature_half)
    rank_scale = lax.rsqrt(slot_adapter_rank.astype(jnp.float32))
    rank_keep = jnp.arange(rank_extent, dtype=jnp.int32)[None, :] < slot_adapter_rank[:, None]
    partial_value = jnp.dot(hidden, key_projection_weight, preferred_element_type=jnp.float32)
    received_rows = lax.all_to_all(outgoing, "rep", split_axis=0, concat_axis=0, tiled=True)
    summed = lax.psum(
        jnp.einsum(
            "khlt,htq->khlq", received_rows, adapter_down_weight, preferred_element_type=jnp.float32
        ),
        "tp",
    )
    reduced_rank_rows = jnp.where(
        rank_keep[None, :, None, :], summed * rank_scale[None, :, None, None], 0.0
    ).astype(jnp.bfloat16)
    sent_back_rows = lax.all_to_all(
        jnp.einsum(
            "pkwb,kbj->pkwj",
            reduced_rank_rows,
            adapter_up_weight,
            preferred_element_type=jnp.float32,
        ).astype(jnp.bfloat16),
        "rep",
        split_axis=0,
        concat_axis=0,
        tiled=True,
    )
    adapter_rows = sent_back_rows.reshape(adapter_number * slot_capacity, key_portion)[
        request_place
    ]
    summed_base = lax.psum(partial_value, "tp")
    replica_portion = lax.dynamic_slice_in_dim(
        summed_base, lax.axis_index("tp") * key_portion, key_portion, 1
    )
    key_output_rows = replica_portion + adapter_rows.astype(jnp.float32)
    return rotary(key_output_rows, lengths, HEAD).astype(jnp.bfloat16)


MESH = pl.DeviceIdType.MESH
WINDOW = 4
TILE = 1024
TURN = 11


def flip(index, mask):
    out = 0
    for bit in (1, 2, 4, 8):
        out = out + (index // bit % 2 + mask // bit % 2) % 2 * bit
    return out


def mask_at(k):
    return k % 2 * (8 + k // 2) + (1 - k % 2) * ((k // 2 * 4 + 6) % 7 + 1)


def keys_kernel(
    n,
    group,
    hidden,
    key_weight,
    down,
    up,
    slots,
    cosine,
    sine,
    out,
    hidden_own,
    key_buf,
    hidden_got,
    slots_got,
    down_got,
    up_got,
    base,
    total,
    totals_got,
    low_got,
    delta,
    delta_got,
    h_send,
    h_recv,
    s_send,
    s_recv,
    d_send,
    d_recv,
    dp_send,
    dp_recv,
    u_send,
    u_recv,
    up_send,
    up_recv,
    t_send,
    t_recv,
    l_send,
    l_recv,
    e_send,
    e_recv,
    own_sem,
    key_sem,
):
    part = lax.axis_index("parts")
    me = lax.axis_index("rep")
    twin = 1 - part
    place = me % group
    first = me - place
    rows, features = hidden.shape
    rank_extent = down.shape[2]
    width = features // group
    depth = features // n
    keys = key_weight.shape[1] // group

    def part_of(j, size):
        return pl.ds(pl.multiple_of(j * size, size), size)

    def remote(source, target, send, recv, p, r):
        return pltpu.make_async_remote_copy(
            src_ref=source,
            dst_ref=target,
            send_sem=send,
            recv_sem=recv,
            device_id=(p, r, 0),
            device_id_type=MESH,
        )

    def hidden_copy(k, to, who, other):
        return remote(
            hidden.at[:, part_of(to % group, width)],
            hidden_got.at[part_of(who % group, rows)],
            h_send.at[k],
            h_recv.at[k],
            part,
            other,
        )

    def slots_copy(k, to, who, other):
        return remote(
            slots,
            slots_got.at[part_of(who % group, rows)],
            s_send.at[k],
            s_recv.at[k],
            part,
            other,
        )

    def down_copy(k, to, who, other):
        return remote(
            down.at[part, part_of(to % group, width)],
            down_got.at[2 * who + part],
            d_send.at[k],
            d_recv.at[k],
            part,
            other,
        )

    def near_copy(k, to, who, other):
        return remote(
            down.at[:, part_of(to % group, width)],
            down_got.at[pl.ds(2 * who, 2)],
            d_send.at[k],
            d_recv.at[k],
            part,
            other,
        )

    def up_copy(k, to, who, other):
        return remote(
            up.at[part, :, part_of(to % group, keys)],
            up_got.at[2 * who + part],
            u_send.at[k],
            u_recv.at[k],
            part,
            other,
        )

    def total_copy(k, to, who, other):
        return remote(
            total.at[part_of(to % group, rows)],
            totals_got.at[who % group],
            t_send.at[k],
            t_recv.at[k],
            part,
            other,
        )

    def low_copy(k, to, who, other):
        return remote(
            low_got.at[who % group],
            low_got.at[who % group],
            l_send.at[k],
            l_recv.at[k],
            part,
            other,
        )

    def delta_copy(k, to, who, other):
        return remote(
            delta.at[to % group],
            delta_got.at[who % group],
            e_send.at[k],
            e_recv.at[k],
            part,
            other,
        )

    def sent(copy, k):
        other = flip(me, k)
        return copy(k, other, me, other)

    def coming(copy, k):
        other = flip(me, k)
        return copy(k, me, other, other)

    def down_pass(k, slot_part):
        at = down_got.at[2 * flip(me, k) + slot_part]
        return remote(at, at, dp_send.at[k], dp_recv.at[k], twin, me)

    def up_pass(k, slot_part):
        at = up_got.at[2 * flip(me, k) + slot_part]
        return remote(at, at, up_send.at[k], up_recv.at[k], twin, me)

    def key_copy(k):
        at = part_of(k, depth)
        return pltpu.make_async_copy(key_weight.at[at], key_buf.at[at], key_sem.at[k])

    barrier = pltpu.get_barrier_semaphore()
    for k in range(1, n):
        pl.semaphore_signal(
            barrier, inc=1, device_id=(part, flip(me, k), 0), device_id_type=MESH
        )
    pl.semaphore_signal(barrier, inc=1, device_id=(twin, me, 0), device_id_type=MESH)

    own = [
        pltpu.make_async_copy(hidden, hidden_own, own_sem.at[0]),
        pltpu.make_async_copy(
            hidden.at[:, part_of(place, width)],
            hidden_got.at[part_of(place, rows)],
            own_sem.at[1],
        ),
        pltpu.make_async_copy(
            down.at[:, part_of(place, width)], down_got.at[pl.ds(2 * me, 2)], own_sem.at[2]
        ),
        pltpu.make_async_copy(
            up.at[:, :, part_of(place, keys)], up_got.at[pl.ds(2 * me, 2)], own_sem.at[3]
        ),
        pltpu.make_async_copy(slots, slots_got.at[part_of(place, rows)], own_sem.at[4]),
    ]
    pl.semaphore_wait(barrier, n)
    for k in range(1, WINDOW + 1):
        sent(down_copy if k % 4 else near_copy, mask_at(k)).start()
    for k in (1, 2, 3):
        sent(hidden_copy, k).start()
    for k in range(1, group):
        sent(slots_copy, k).start()
    for copy in own:
        copy.start()
    for k in range(n):
        key_copy(k).start()

    total[...] = jnp.zeros_like(total)
    base[...] = jnp.zeros_like(base)

    def base_step(k):
        key_copy(k).wait()
        at = part_of(k, depth)
        base[...] += jnp.dot(
            hidden_own[:, at], key_buf[at, :], preferred_element_type=jnp.float32
        )

    def pass_down(k):
        mask = mask_at(k)

        @pl.when(k % 4 > 0)
        def _():
            coming(down_copy, mask).wait_recv()
            down_pass(mask, part).start()

        @pl.when(k % 4 == 0)
        def _():
            coming(near_copy, mask).wait_recv()

        later = k + WINDOW

        @pl.when((later < n) & (later % 4 > 0))
        def _():
            sent(down_copy, mask_at(later)).start()

        @pl.when((later < n) & (later % 4 == 0))
        def _():
            sent(near_copy, mask_at(later)).start()

        base_step(k)

    def shrink_pair(s):
        low_slot = (2 * s).astype(jnp.float32)

        def tile(j, carry):
            at = part_of(j, TILE)
            slot = slots_got[at, :].astype(jnp.float32)
            weight = jnp.concatenate([down_got[2 * s], down_got[2 * s + 1]], axis=1)
            product = jnp.dot(hidden_got[at, :], weight, preferred_element_type=jnp.float32)
            total[at, :] = jnp.where(
                slot == low_slot,
                product[:, :rank_extent],
                jnp.where(slot == low_slot + 1.0, product[:, rank_extent:], total[at, :]),
            )
            return carry

        lax.fori_loop(0, group * rows // TILE, tile, 0)

    def shrink_step(k, carry):
        mask = mask_at(k)

        @pl.when(k % 4 > 0)
        def _():
            down_pass(mask, twin).wait_recv()

        shrink_pair(flip(me, mask))
        return carry

    def first_steps(k, carry):
        pass_down(k)

        @pl.when(k % 2 * (8 // (k + 1)) >= 1)
        def _():
            sent(hidden_copy, 4 + k // 2).start()

        return carry

    def last_steps(k, carry):
        pass_down(k)
        shrink_step(2 * (k - TURN) - 1, 0)
        shrink_step(2 * (k - TURN), 0)
        return carry

    own[0].wait()
    base_step(0)
    lax.fori_loop(1, TURN + 1, first_steps, 0)
    for k in range(1, n):
        sent(up_copy, k).start()
    for copy in own[1:]:
        copy.wait()
    for k in range(1, group):
        coming(slots_copy, k).wait_recv()
        coming(hidden_copy, k).wait_recv()
    shrink_pair(me)
    lax.fori_loop(TURN + 1, n, last_steps, 0)
    lax.fori_loop(2 * (n - 1 - TURN) + 1, n, shrink_step, 0)
    for k in range(1, group):
        sent(total_copy, k).start()

    def pass_up(k, carry):
        mask = mask_at(k)
        coming(up_copy, mask).wait_recv()
        up_pass(mask, part).start()
        return carry

    lax.fori_loop(1, n, pass_up, 0)

    def wait_passed_up(k, carry):
        up_pass(mask_at(k), twin).wait_recv()
        return carry

    lax.fori_loop(1, n, wait_passed_up, 0)

    own_slot = slots_got[part_of(place, rows), :].astype(jnp.float32)

    def find_rank(s, rank):
        here = up_got[s, rank_extent : rank_extent + 16, :].astype(jnp.float32)[0:1, :]
        return jnp.where(own_slot == s.astype(jnp.float32), here, rank)

    rank = lax.fori_loop(0, 2 * n, find_rank, jnp.ones((rows, rank_extent), jnp.float32))
    feature = lax.broadcasted_iota(jnp.int32, (rows, rank_extent), 1).astype(jnp.float32)
    shrink = total[part_of(place, rows), :]
    for k in range(1, group):
        coming(total_copy, k).wait_recv()
        shrink = shrink + totals_got[flip(place, k)]
    low_got[place] = jnp.where(feature < rank, shrink * lax.rsqrt(rank), 0.0).astype(jnp.bfloat16)
    for k in range(1, group):
        sent(low_copy, k).start()

    def expand_block(j):
        slot = slots_got[part_of(j, rows), :].astype(jnp.float32)
        low = low_got[j].astype(jnp.float32)

        def pair(s, sum_so_far):
            low_slot = (2 * s).astype(jnp.float32)
            spread = jnp.concatenate(
                [
                    jnp.where(slot == low_slot, low, 0.0).astype(jnp.bfloat16),
                    jnp.where(slot == low_slot + 1.0, low, 0.0).astype(jnp.bfloat16),
                ],
                axis=1,
            )
            weight = jnp.concatenate(
                [up_got[2 * s, :rank_extent, :], up_got[2 * s + 1, :rank_extent, :]], axis=0
            )
            return sum_so_far + jnp.dot(spread, weight, preferred_element_type=jnp.float32)

        delta[j] = lax.fori_loop(
            0, n, pair, jnp.zeros((rows, keys), jnp.float32), unroll=4
        ).astype(jnp.bfloat16)

    def expand_step(k, carry):
        coming(low_copy, k).wait_recv()
        expand_block(flip(place, k))
        sent(delta_copy, k).start()
        return carry

    def rotate(j, values):
        at = part_of(j, keys)
        pre = base[:, at] + values.astype(jnp.float32)
        turned = pltpu.roll(pre, keys // 2, axis=1)
        out[:, at] = (pre * cosine[...] + turned * sine[...]).astype(out.dtype)

    def rotate_step(k, carry):
        coming(delta_copy, k).wait_recv()
        j = flip(place, k)
        rotate(j, delta_got[j])
        return carry

    lax.fori_loop(1, group, expand_step, 0)
    expand_block(place)
    rotate(place, delta[place])
    lax.fori_loop(1, group, rotate_step, 0)

    for k in range(1, group):
        for copy in (hidden_copy, slots_copy, total_copy, low_copy, delta_copy):
            sent(copy, k).wait_send()
    for k in range(1, n):
        if k < 4:
            sent(near_copy, k).wait_send()
        else:
            sent(down_copy, k).wait_send()
            down_pass(k, part).wait_send()
        sent(up_copy, k).wait_send()
        up_pass(k, part).wait_send()


def keys_call(hidden, key_weight, down, up, slots, cosine, sine):
    n = lax.axis_size("rep")
    group = n // 2
    rows, features = hidden.shape
    rank_extent = down.shape[2]
    width = features // group
    keys = key_weight.shape[1]
    key_block = keys // group
    any_space = pl.BlockSpec(memory_space=pl.ANY)
    vmem = pl.BlockSpec(memory_space=pltpu.VMEM)
    half, full = jnp.bfloat16, jnp.float32
    dma = pltpu.SemaphoreType.DMA
    return pl.pallas_call(
        functools.partial(keys_kernel, n, group),
        out_shape=jax.ShapeDtypeStruct((rows, keys), half),
        in_specs=[any_space] * 5 + [vmem] * 2,
        out_specs=vmem,
        scratch_shapes=[
            pltpu.VMEM((rows, features), half),
            pltpu.VMEM((features, keys), half),
            pltpu.VMEM((group * rows, width), half),
            pltpu.VMEM((group * rows, rank_extent), half),
            pltpu.VMEM((2 * n, width, rank_extent), half),
            pltpu.VMEM((2 * n, up.shape[1], key_block), half),
            pltpu.VMEM((rows, keys), full),
            pltpu.VMEM((group * rows, rank_extent), full),
            pltpu.VMEM((group, rows, rank_extent), full),
            pltpu.VMEM((group, rows, rank_extent), half),
            pltpu.VMEM((group, rows, key_block), half),
            pltpu.VMEM((group, rows, key_block), half),
        ]
        + [dma((group,))] * 4
        + [dma((n,))] * 8
        + [dma((group,))] * 6
        + [dma((5,)), dma((n,))],
        compiler_params=pltpu.CompilerParams(
            collective_id=0, has_side_effects=True, vmem_limit_bytes=56 * 2**20
        ),
        cost_estimate=pl.CostEstimate(
            flops=2 * rows * features * keys + 4 * rows * features * n * rank_extent,
            bytes_accessed=2 * features * (rows + keys + 2 * rank_extent),
            transcendentals=0,
        ),
    )(hidden, key_weight, down, up, slots, cosine, sine)


def shared(
    hidden,
    request_adapter,
    lengths,
    key_projection_weight,
    adapter_down_weight,
    adapter_up_weight,
    slot_adapter_rank,
    placement,
):
    rows = hidden.shape[0]
    adapters = placement.shape[0]
    rank_extent = adapter_down_weight.shape[2]
    numbers = jnp.arange(adapters, dtype=jnp.int32)[None, :]
    slot_ids = jnp.sum(jnp.where(request_adapter == numbers, placement[None, :], 0), axis=1)
    slots = jnp.broadcast_to(slot_ids[:, None].astype(jnp.bfloat16), (rows, rank_extent))
    ranks = jnp.broadcast_to(
        slot_adapter_rank.astype(jnp.bfloat16)[:, None, None],
        (slot_adapter_rank.shape[0], 16, adapter_up_weight.shape[2]),
    )
    up = jnp.concatenate([adapter_up_weight, ranks], axis=1)
    half_size = HEAD // 2
    inverse = jnp.exp(
        jnp.arange(half_size, dtype=jnp.float32) * (-2.0 * math.log(10000.0) / HEAD)
    )
    angles = lengths.astype(jnp.float32)[:, None] * inverse[None, :]
    cosine, sine = jnp.cos(angles), jnp.sin(angles)
    return keys_call(
        hidden,
        key_projection_weight,
        adapter_down_weight,
        up,
        slots,
        jnp.concatenate([cosine, cosine], axis=1),
        jnp.concatenate([-sine, sine], axis=1),
    )


def solution(mesh):
    sizes = dict(mesh.shape)
    fits = sizes["parts"] == 2 and sizes["tp"] == 1 and sizes["rep"] == 16
    on_device = shared if fits else routed
    in_specs = (
        P(("parts", "rep"), "tp"),
        P(("parts", "rep"), None),
        P(("parts", "rep")),
        P("tp", None),
        P("rep", "tp", None),
        P("rep", None, "tp"),
        P("rep"),
        P(),
    )
    out_specs = P(("parts", "rep"), "tp")
    return jax.shard_map(
        on_device, mesh=mesh, in_specs=in_specs, out_specs=out_specs, check_vma=False
    )
```
